256 devices in a mesh: dp: 64 (over y, z, core), mp: 4 (over x).
Axes of the slice: x: 4, y: 4, z: 8, core: 2. Of those that a mesh axis runs over, the one named last changes fastest.
Arguments:
- features: bfloat16 [32768, 8192], P('dp', 'mp'), may hold values from -6 to 6
- up_cotangent: bfloat16 [32768, 14336], P('dp', 'mp'), may hold values from -0.032958984 to 0.032958984
- proj_basis: bfloat16 [8192, 512], P('mp'), may hold values from -0.0625 to 0.0625
- first_moment: float32 [512, 14336], P('dp', 'mp'), may hold values from -3 to 3
- second_moment: float32 [512, 14336], P('dp', 'mp'), may hold values from 0.0001 to 0.01
Outputs:
- weight_update: float32 [8192, 14336], P('dp', 'mp')
- new_first: float32 [512, 14336], P('dp', 'mp')
- new_second: float32 [512, 14336], P('dp', 'mp')
The draws below stay inside these ranges and needn't reach their ends.
All inputs are finite; a program needn't handle non-finite values.
Results may differ from the reference program's by a relative error of at most 0.0041.
Values may be sent and summed in bfloat16 or wider, within the bound.
A program may use at most 64 MiB of HBM per device.

```python
import math
import jax
import jax.numpy as jnp

D = 8192
FF_WIN = 14336
RANK = 512
STEP = 10
TOK_DEV = 512
TOKENS = 32768
N_DP = 64


def level_of(key, dims, pieces, least, top_value):
    level, own = 1.0, jax.random.fold_in(key, 6)
    for position, shards_of in pieces:
        heights = jnp.exp(jax.random.uniform(jax.random.fold_in(own, position), (shards_of,), jnp.float32, least / len(pieces), top_value / len(pieces)))
        level = level * jnp.repeat(heights, dims[position] // shards_of).reshape([-1 if axis == position else 1 for axis in range(len(dims))])
    return level


def centred(own_key, dims, width, limit, shards=(), dtype=jnp.bfloat16):
    drawn = width * jax.random.normal(own_key, dims, jnp.float32)
    if shards:
        drawn = drawn * level_of(own_key, dims, shards, -0.22, 0.18)
    return jnp.clip(drawn, -limit, limit).astype(dtype)


def setup_inputs(seed: int = 0) -> dict:
    keys = jax.random.split(jax.random.key(seed), 6)
    features = centred(keys[0], (TOKENS, D), 1.0, 6.0, ((0, 64), (1, 4)))
    up_cotangent = centred(keys[1], (TOKENS, FF_WIN), ((TOK_DEV * N_DP) ** -0.5), 0.032958984, ((0, 64), (1, 4)))
    proj_basis = centred(keys[2], (D, RANK), D ** -0.5, 0.0625, ((0, 4),))
    first_moment = centred(keys[3], (RANK, FF_WIN), 0.5, 3.0, ((0, 64), (1, 4)), jnp.float32)
    second_moment = jnp.clip(jnp.exp(math.log(0.01) - 4.6051702 * jax.random.uniform(keys[4], (RANK, FF_WIN), jnp.float32) ** level_of(keys[4], (RANK, FF_WIN), ((0, 64), (1, 4)), -0.2, 0.2)), 0.0001, 0.01)
    return {"features": features, "up_cotangent": up_cotangent, "proj_basis": proj_basis, "first_moment": first_moment, "second_moment": second_moment}


def reference(features, up_cotangent, proj_basis, first_moment, second_moment):
    coeffs = jnp.dot(features, proj_basis, preferred_element_type=jnp.float32).astype(jnp.bfloat16)
    low_grad = jnp.dot(coeffs.T, up_cotangent, preferred_element_type=jnp.float32)
    new_first = 0.9 * first_moment + 0.1 * low_grad
    new_second = 0.999 * second_moment + 0.001 * low_grad * low_grad
    first_hat = new_first / (1.0 - 0.9 ** STEP)
    second_hat = new_second / (1.0 - 0.999 ** STEP)
    direction = (first_hat / (jnp.sqrt(second_hat) + 1e-08)).astype(jnp.bfloat16)
    weight_update = 0.25 * jnp.dot(proj_basis, direction, preferred_element_type=jnp.float32)
    return (weight_update, new_first, new_second)
```

```python
import jax
import jax.numpy as jnp
from jax import lax
from jax.experimental import pallas as pl
from jax.experimental.pallas import tpu as pltpu
from jax.sharding import PartitionSpec as P

STEP = 10
NX, NY, NZ = 4, 4, 8
COLS = 3584
WIDTHS = (512, 512, 512, 512, 512, 512, 512)
STARTS = tuple(sum(WIDTHS[:i]) for i in range(len(WIDTHS)))
NCH = len(WIDTHS)
WMAX = max(WIDTHS)
KB = 4
F32, BF16 = jnp.float32, jnp.bfloat16


def adam_rows(first_moment, second_moment, low_grad):
    new_first = 0.9 * first_moment + 0.1 * low_grad
    new_second = 0.999 * second_moment + 0.001 * low_grad * low_grad
    first_hat = new_first / (1.0 - 0.9**STEP)
    second_hat = new_second / (1.0 - 0.999**STEP)
    direction = first_hat / (jnp.sqrt(second_hat) + 1e-08)
    return (new_first, new_second, direction)


def kernel(
    f_hbm, u_hbm, b_hbm, m_hbm, v_hbm,
    w_hbm, nm_hbm, nv_hbm,
    fv, bv, u, mv, vv, nm, nv,
    acc, pt, xs, xr, qv, ct,
    lf, ys, yr, zf, zs, zr, db, br, be, wo,
    ld_f, ld_b, ld_u, ld_m, st_o, st_m,
    sx, rx, sq, rq, su, ru, sb, rb,
    sy, ry, sz, rz, sg, rg, sh, rh, sk, rk,
):
    dp = lax.axis_index("dp")
    x = lax.axis_index("mp")
    c = lax.rem(dp, 2)
    z = lax.rem(dp // 2, NZ)
    y = dp // (2 * NZ)
    oc = 1 - c

    def dev(x_, y_, z_, c_):
        return ((y_ * NZ + z_) * 2 + c_, x_)

    def send(src, dst, ss, rs, to):
        return pltpu.make_async_remote_copy(
            src_ref=src, dst_ref=dst, send_sem=ss, recv_sem=rs,
            device_id=to, device_id_type=pl.DeviceIdType.MESH,
        )

    xd = [lax.rem(x + d, NX) for d in range(NX)]
    yd = [lax.rem(y + d, NY) for d in range(NY)]
    zd = [lax.rem(z + d, NZ) for d in range(NZ)]
    sib = dev(x, y, z, oc)

    kw = fv.shape[2]
    lf_c = [pltpu.make_async_copy(f_hbm.at[:, pl.ds(k * kw, kw)], fv.at[k], ld_f.at[k]) for k in range(KB)]
    lb_c = [pltpu.make_async_copy(b_hbm.at[pl.ds(k * kw, kw), :], bv.at[k], ld_b.at[k]) for k in range(KB)]
    for k in range(KB):
        lb_c[k].start()
        lf_c[k].start()
    lu = pltpu.make_async_copy(u_hbm, u.at[c], ld_u)
    lu.start()
    lm = pltpu.make_async_copy(m_hbm, mv, ld_m.at[0])
    lv = pltpu.make_async_copy(v_hbm, vv, ld_m.at[1])
    lm.start()
    lv.start()

    bar = pltpu.get_barrier_semaphore()
    peers = [sib]
    for d in range(1, NX):
        peers += [dev(xd[d], y, z, c), dev(xd[d], y, z, oc)]
    peers += [dev(x, yd[d], z, c) for d in range(1, NY)]
    peers += [dev(x, y, zd[d], c) for d in range(1, NZ)]
    for p in peers:
        pl.semaphore_signal(bar, inc=1, device_id=p, device_id_type=pl.DeviceIdType.MESH)

    for k in range(KB):
        lb_c[k].wait()
        lf_c[k].wait()
        part = jnp.dot(fv[k], bv[k], preferred_element_type=F32)
        if k == 0:
            acc[...] = part
        else:
            acc[...] += part
    for yy in range(NY):
        tt = acc[:, yy * 128:(yy + 1) * 128].T
        for h in range(2):
            for zl in range(4):
                for cc in range(2):
                    r = ((h * 4 + zl) * 2 + cc) * 8
                    pt[2 * cc + h, yy * 32 + zl * 8:yy * 32 + zl * 8 + 8, :] = tt[r:r + 8, :]
    xs[...] = pt[...].astype(BF16)

    pl.semaphore_wait(bar, len(peers))
    cx = [send(xs.at[xd[d]], xr.at[d - 1], sx.at[d - 1], rx.at[d - 1], dev(xd[d], y, z, c)) for d in range(1, NX)]
    for cp in cx:
        cp.start()
    cu = send(u_hbm, u.at[c], su, ru, sib)
    cu.start()
    cu_in = send(u_hbm, u.at[oc], su, ru, sib)

    for cp in cx:
        cp.wait_recv()
    q = pt[x]
    for d in range(NX - 1):
        q = q + xr[d].astype(F32)
    hx = lax.rem(x, 2)
    cq = x // 2
    qv[...] = q.astype(BF16)
    cqs = [send(qv, ct.at[c, hx], sq.at[d], rq.at[c, hx], dev(xd[d], y, z, cq)) for d in range(NX)]
    for d in range(1, NX):
        cqs[d].start()

    @pl.when(cq != c)
    def _():
        cqs[0].start()

    @pl.when(cq == c)
    def _():
        ct[c, hx] = qv[...]

    rows = br.shape[0]
    brow = lax.rem(dp, 16)
    src_b = bv.at[brow // 4, pl.ds(pl.multiple_of(lax.rem(brow, 4) * rows, rows), rows), :]
    cbs = [send(src_b, br, sb.at[d - 1], rb, dev(xd[d], y, z, c)) for d in range(1, NX)]

    @pl.when(x == y)
    def _():
        for cp in cbs:
            cp.start()
        loc = pltpu.make_async_copy(src_b, br, rb)
        loc.start()
        loc.wait()

    @pl.when(x != y)
    def _():
        cbs[0].wait_recv()

    ri = lax.broadcasted_iota(jnp.int32, (512, 512), 0)
    ji = lax.broadcasted_iota(jnp.int32, (512, 512), 1)
    jl = lax.broadcasted_iota(jnp.int32, (rows, 512), 1)
    for cc in range(2):
        e = (ri == (ji & ~8) + cc * 8).astype(F32).astype(BF16)
        t = jnp.dot(br[...], e, preferred_element_type=F32)
        for s in range(2):
            be[s, :, cc * 512:(cc + 1) * 512] = jnp.where(((jl >> 3) & 1) == s, t, 0.0).astype(BF16)

    for cc in range(2):
        for h in range(2):
            own = (2 * c + h == x) & (c == cc)
            cp = send(ct.at[cc, h], ct.at[cc, h], sq.at[0], rq.at[cc, h], sib)

            @pl.when(jnp.logical_not(own))
            def _():
                cp.wait_recv()
    lu.wait()
    cu_in.wait_recv()
    lm.wait()
    lv.wait()

    def y_copies(k):
        w = WIDTHS[k]
        return [
            send(ys.at[k, yd[d], :, pl.ds(0, w)], yr.at[k, d - 1, :, pl.ds(0, w)], sy.at[k, d - 1], ry.at[k, d - 1], dev(x, yd[d], z, c))
            for d in range(1, NY)
        ]

    def z_copies(k):
        w = WIDTHS[k] // 2
        return [
            send(zs.at[k, zd[d], :, pl.ds(0, w)], zr.at[k, d - 1, :, pl.ds(0, w)], sz.at[k, d - 1], rz.at[k, d - 1], dev(x, y, zd[d], c))
            for d in range(1, NZ)
        ]

    def gz_copies(k):
        w = WIDTHS[k] // 2
        mine = db.at[k, c, y, z, :, pl.ds(0, w)]
        out = [send(mine, mine, sg.at[k, d - 1], rg.at[k, d - 1], dev(x, y, zd[d], c)) for d in range(1, NZ)]
        inn = []
        for d in range(1, NZ):
            zz = lax.rem(z + NZ - d, NZ)
            theirs = db.at[k, c, y, zz, :, pl.ds(0, w)]
            inn.append(send(theirs, theirs, sg.at[k, d - 1], rg.at[k, d - 1], dev(x, y, zz, c)))
        return out, inn

    def gy_copies(k):
        w = WIDTHS[k] // 2
        blk = lambda yy: db.at[k, c, yy, :, :, pl.ds(0, w)]
        lo = lambda yy: db.at[k, c, yy, pl.ds(0, 4), :, pl.ds(0, w)]
        hi = lambda yy: db.at[k, c, yy, pl.ds(4, 4), :, pl.ds(0, w)]
        up, dn = dev(x, yd[1], z, c), dev(x, yd[3], z, c)
        first = [
            send(blk(y), blk(y), sh.at[k, 0], rh.at[k, 0], up),
            send(blk(y), blk(y), sh.at[k, 1], rh.at[k, 1], dn),
        ]
        first_in = [
            send(blk(yd[3]), blk(yd[3]), sh.at[k, 0], rh.at[k, 0], up),
            send(blk(yd[1]), blk(yd[1]), sh.at[k, 1], rh.at[k, 1], dn),
        ]
        second = [
            send(lo(yd[3]), lo(yd[3]), sh.at[k, 2], rh.at[k, 2], up),
            send(hi(yd[1]), hi(yd[1]), sh.at[k, 3], rh.at[k, 3], dn),
        ]
        second_in = [
            send(lo(yd[2]), lo(yd[2]), sh.at[k, 2], rh.at[k, 2], up),
            send(hi(yd[2]), hi(yd[2]), sh.at[k, 3], rh.at[k, 3], dn),
        ]
        return first, first_in, second, second_in

    def k_copies(k):
        w = WIDTHS[k] // 2
        blk = lambda cc, yy: db.at[k, cc, yy, :, :, pl.ds(0, w)]
        out = [send(blk(c, yd[d]), blk(c, yd[d]), sk.at[k, d], rk.at[k, d], sib) for d in range(NY)]
        inn = [send(blk(oc, yd[d]), blk(oc, yd[d]), sk.at[k, d], rk.at[k, d], sib) for d in range(NY)]
        return out, inn

    def out_copy(k):
        sl = pl.ds(STARTS[k], WIDTHS[k])
        return pltpu.make_async_copy(wo.at[:, sl], w_hbm.at[:, sl], st_o.at[k])

    def s1(k):
        s0, w = STARTS[k], WIDTHS[k]
        for h in range(2):
            l = jnp.dot(ct[0, h], u[0, :, s0:s0 + w], preferred_element_type=F32)
            l += jnp.dot(ct[1, h], u[1, :, s0:s0 + w], preferred_element_type=F32)
            for yy in range(NY):
                part = l[yy * 32:(yy + 1) * 32]
                lf[yy, h * 32:(h + 1) * 32, s0:s0 + w] = part
                ys[k, yy, h * 32:(h + 1) * 32, 0:w] = part.astype(BF16)
        for cp in y_copies(k):
            cp.start()

    def s2(k):
        s0, w = STARTS[k], WIDTHS[k]
        for cp in y_copies(k):
            cp.wait_recv()
        g = lf[y, :, s0:s0 + w]
        for d in range(NY - 1):
            g = g + yr[k, d, :, 0:w].astype(F32)
        for zz in range(NZ):
            part = g[zz * 8:(zz + 1) * 8]
            zf[zz, :, s0:s0 + w] = part
            zs[k, zz, :, 0:w // 2] = jnp.concatenate([part[:, :w // 2], part[:, w // 2:]], axis=0).astype(BF16)
        for cp in z_copies(k):
            cp.start()

    def s3(k):
        s0, w = STARTS[k], WIDTHS[k]
        for cp in z_copies(k):
            cp.wait_recv()
        t = zr[k, 0, :, 0:w // 2].astype(F32)
        for d in range(1, NZ - 1):
            t = t + zr[k, d, :, 0:w // 2].astype(F32)
        g = zf[z, :, s0:s0 + w] + jnp.concatenate([t[0:8], t[8:16]], axis=1)
        a, b, dr = adam_rows(mv[:, s0:s0 + w], vv[:, s0:s0 + w], g)
        nm[:, s0:s0 + w] = a
        nv[:, s0:s0 + w] = b
        db[k, c, y, z, :, 0:w // 2] = jnp.concatenate([dr[:, :w // 2], dr[:, w // 2:]], axis=0).astype(BF16)
        for cp in gz_copies(k)[0]:
            cp.start()

    def s4(k):
        for cp in gz_copies(k)[1]:
            cp.wait_recv()
        for cp in gy_copies(k)[0]:
            cp.start()
        k_copies(k)[0][0].start()

    def s5(k):
        _, first_in, second, _ = gy_copies(k)
        out = k_copies(k)[0]
        first_in[0].wait_recv()
        second[0].start()
        first_in[1].wait_recv()
        second[1].start()
        out[3].start()
        out[1].start()

    def s6(k):
        for cp in gy_copies(k)[3]:
            cp.wait_recv()
        k_copies(k)[0][2].start()

    def s7(k):
        s0, w = STARTS[k], WIDTHS[k]
        for cp in k_copies(k)[1]:
            cp.wait_recv()
        d_all = db[k, :, :, :, :, 0:w // 2].reshape(1024, w // 2)
        for s in range(2):
            o = s0 + s * (w // 2)
            wo[:, o:o + w // 2] = 0.25 * jnp.dot(be[s], d_all, preferred_element_type=F32)
        out_copy(k).start()

    om = [pltpu.make_async_copy(nm, nm_hbm, st_m.at[0]), pltpu.make_async_copy(nv, nv_hbm, st_m.at[1])]
    stages = [s1, s2, s3, s4, s5, s6, s7]
    for k in range(NCH):
        s1(k)
    for t in range(NCH + len(stages) - 2):
        for i in range(len(stages) - 1, 0, -1):
            k = t - (i - 1)
            if 0 <= k < NCH:
                stages[i](k)
                if i == 2 and k == NCH - 1:
                    om[0].start()
                    om[1].start()

    for cp in cx:
        cp.wait_send()
    cu.wait_send()
    for d in range(1, NX):
        cqs[d].wait_send()

    @pl.when(cq != c)
    def _():
        cqs[0].wait_send()

    @pl.when(x == y)
    def _():
        for cp in cbs:
            cp.wait_send()

    for k in range(NCH):
        first, _, second, _ = gy_copies(k)
        for cp in y_copies(k) + z_copies(k) + gz_copies(k)[0] + first + second + k_copies(k)[0]:
            cp.wait_send()
        out_copy(k).wait()
    om[0].wait()
    om[1].wait()


def body(features, up_cotangent, proj_basis, first_moment, second_moment):
    tok, feat = features.shape
    depth, rank = proj_basis.shape
    cols = up_cotangent.shape[1]
    kw = feat // KB
    rows = 128
    dma = pltpu.SemaphoreType.DMA
    anyspec = pl.BlockSpec(memory_space=pl.ANY)
    wu, nf, ns = pl.pallas_call(
        kernel,
        out_shape=(
            jax.ShapeDtypeStruct((rows, cols), F32),
            jax.ShapeDtypeStruct(first_moment.shape, F32),
            jax.ShapeDtypeStruct(second_moment.shape, F32),
        ),
        in_specs=[anyspec] * 5,
        out_specs=(anyspec,) * 3,
        scratch_shapes=[
            pltpu.VMEM((KB, tok, kw), BF16),
            pltpu.VMEM((KB, kw, rank), BF16),
            pltpu.VMEM((2, tok, cols), BF16),
            pltpu.VMEM((8, cols), F32),
            pltpu.VMEM((8, cols), F32),
            pltpu.VMEM((8, cols), F32),
            pltpu.VMEM((8, cols), F32),
            pltpu.VMEM((tok, rank), F32),
            pltpu.VMEM((NX, 128, tok), F32),
            pltpu.VMEM((NX, 128, tok), BF16),
            pltpu.VMEM((NX - 1, 128, tok), BF16),
            pltpu.VMEM((128, tok), BF16),
            pltpu.VMEM((2, 2, 128, tok), BF16),
            pltpu.VMEM((NY, 64, cols), F32),
            pltpu.VMEM((NCH, NY, 64, WMAX), BF16),
            pltpu.VMEM((NCH, NY - 1, 64, WMAX), BF16),
            pltpu.VMEM((NZ, 8, cols), F32),
            pltpu.VMEM((NCH, NZ, 16, WMAX // 2), BF16),
            pltpu.VMEM((NCH, NZ - 1, 16, WMAX // 2), BF16),
            pltpu.VMEM((NCH, 2, NY, NZ, 16, WMAX // 2), BF16),
            pltpu.VMEM((rows, rank), BF16),
            pltpu.VMEM((2, rows, 2 * rank), BF16),
            pltpu.VMEM((rows, cols), F32),
            dma((KB,)), dma((KB,)), dma(()), dma((2,)), dma((NCH,)), dma((2,)),
            dma((3,)), dma((3,)), dma((4,)), dma((2, 2)), dma(()), dma(()), dma((3,)), dma(()),
            dma((NCH, 3)), dma((NCH, 3)), dma((NCH, 7)), dma((NCH, 7)), dma((NCH, 7)), dma((NCH, 7)),
            dma((NCH, 4)), dma((NCH, 4)), dma((NCH, 4)), dma((NCH, 4)),
        ],
        compiler_params=pltpu.CompilerParams(
            collective_id=0, has_side_effects=True, vmem_limit_bytes=56 * 2**20
        ),
        cost_estimate=pl.CostEstimate(flops=4 * 10**9, bytes_accessed=12 * 10**6, transcendentals=0),
        name="galore",
    )(features, up_cotangent, proj_basis, first_moment, second_moment)
    return (wu, nf, ns)


def solution(mesh):
    return jax.shard_map(
        body,
        mesh=mesh,
        in_specs=(P("dp", "mp"), P("dp", "mp"), P("mp", None), P("dp", "mp"), P("dp", "mp")),
        out_specs=(P("dp", "mp"), P("dp", "mp"), P("dp", "mp")),
        check_vma=False,
    )
```

```python
import jax
import jax.numpy as jnp
from jax import lax
from jax.experimental import pallas as pl
from jax.experimental.pallas import tpu as pltpu
from jax.sharding import PartitionSpec as P

STEP = 10
PACE = 1.3
LATENCY = (3.5, 5.5, 5.5, 4.0, 4.0, 2.0, 0.0)
PARTS = (pl.ds(0, 1), pl.ds(1, 3))
NX, NY, NZ = 4, 4, 8
COLS = 3584
WIDTHS = (512, 512, 512, 512, 512, 512, 512)
STARTS = tuple(sum(WIDTHS[:i]) for i in range(len(WIDTHS)))
NCH = len(WIDTHS)
WMAX = max(WIDTHS)
KB = 4
F32, BF16 = jnp.float32, jnp.bfloat16


def adam_rows(first_moment, second_moment, low_grad):
    new_first = 0.9 * first_moment + 0.1 * low_grad
    new_second = 0.999 * second_moment + 0.001 * low_grad * low_grad
    first_hat = new_first / (1.0 - 0.9**STEP)
    second_hat = new_second / (1.0 - 0.999**STEP)
    direction = first_hat / (jnp.sqrt(second_hat) + 1e-08)
    return (new_first, new_second, direction)


def kernel(
    f_hbm, u_hbm, b_hbm, m_hbm, v_hbm,
    wo, nm, nv,
    fv, bv, u, mv, vv,
    acc, pt, xs, xr, qv, ct,
    lf, ys, yr, zf, zs, zr, db, br, be,
    ld_f, ld_b, ld_u, ld_m,
    sx, rx, sq, rq, su, ru, sb, rb,
    sy, ry, sz, rz, sg, rg, sh, rh, sk, rk,
):
    dp = lax.axis_index("dp")
    x = lax.axis_index("mp")
    c = lax.rem(dp, 2)
    z = lax.rem(dp // 2, NZ)
    y = dp // (2 * NZ)
    oc = 1 - c

    def dev(x_, y_, z_, c_):
        return ((y_ * NZ + z_) * 2 + c_, x_)

    def send(src, dst, ss, rs, to):
        return pltpu.make_async_remote_copy(
            src_ref=src, dst_ref=dst, send_sem=ss, recv_sem=rs,
            device_id=to, device_id_type=pl.DeviceIdType.MESH,
        )

    xd = [lax.rem(x + d, NX) for d in range(NX)]
    yd = [lax.rem(y + d, NY) for d in range(NY)]
    zd = [lax.rem(z + d, NZ) for d in range(NZ)]
    yo = [yd[2], yd[1], yd[3], yd[0]]
    sib = dev(x, y, z, oc)

    kw = fv.shape[2]
    lf_c = [pltpu.make_async_copy(f_hbm.at[:, pl.ds(k * kw, kw)], fv.at[k], ld_f.at[k]) for k in range(KB)]
    lb_c = [pltpu.make_async_copy(b_hbm.at[pl.ds(k * kw, kw), :], bv.at[k], ld_b.at[k]) for k in range(KB)]
    for k in range(KB):
        lb_c[k].start()
        lf_c[k].start()
    lu = pltpu.make_async_copy(u_hbm, u.at[c], ld_u)
    lu.start()
    lm = pltpu.make_async_copy(m_hbm, mv, ld_m.at[0])
    lv = pltpu.make_async_copy(v_hbm, vv, ld_m.at[1])
    lm.start()
    lv.start()

    bar = pltpu.get_barrier_semaphore()
    peers = [sib]
    for d in range(1, NX):
        peers += [dev(xd[d], y, z, c), dev(xd[d], y, z, oc)]
    peers += [dev(x, yd[d], z, c) for d in range(1, NY)]
    peers += [dev(x, y, zd[d], c) for d in range(1, NZ)]
    for p in peers:
        pl.semaphore_signal(bar, inc=1, device_id=p, device_id_type=pl.DeviceIdType.MESH)

    for k in range(KB):
        lb_c[k].wait()
        lf_c[k].wait()
        part = jnp.dot(fv[k], bv[k], preferred_element_type=F32)
        if k == 0:
            acc[...] = part
        else:
            acc[...] += part
    for yy in range(NY):
        tt = acc[:, yy * 128:(yy + 1) * 128].T
        for h in range(2):
            for zl in range(4):
                for cc in range(2):
                    r = ((h * 4 + zl) * 2 + cc) * 8
                    pt[2 * cc + h, yy, zl * 8:zl * 8 + 8, :] = tt[r:r + 8, :]
    for j in range(NY):
        for xx in range(NX):
            xs[xx, j] = pt[xx, yo[j]].astype(BF16)

    pl.semaphore_wait(bar, len(peers))
    cx = [
        [
            send(xs.at[xd[d], sl], xr.at[d - 1, sl], sx.at[p, d - 1], rx.at[p, d - 1], dev(xd[d], y, z, c))
            for d in range(1, NX)
        ]
        for p, sl in enumerate(PARTS)
    ]
    for p in range(2):
        for cp in cx[p]:
            cp.start()
    cu = send(u_hbm, u.at[c], su, ru, sib)
    cu.start()
    cu_in = send(u_hbm, u.at[oc], su, ru, sib)

    hx = lax.rem(x, 2)
    cq = x // 2

    def q_copies(p):
        sl = PARTS[p]
        return [send(qv.at[sl], ct.at[c, hx, sl], sq.at[p, d], rq.at[p, c, hx], dev(xd[d], y, z, cq)) for d in range(NX)]

    def x_reduce(p):
        for cp in cx[p]:
            cp.wait_recv()
        for j in (0,) if p == 0 else (1, 2, 3):
            q = pt[x, yo[j]]
            for d in range(NX - 1):
                q = q + xr[d, j].astype(F32)
            qv[j] = q.astype(BF16)
        cps = q_copies(p)
        for d in range(1, NX):
            cps[d].start()

        @pl.when(cq != c)
        def _():
            cps[0].start()

        @pl.when(cq == c)
        def _():
            for j in (0,) if p == 0 else (1, 2, 3):
                ct[c, hx, j] = qv[j]

    def x_gathered(p):
        sl = PARTS[p]
        for cc in range(2):
            for h in range(2):
                own = (2 * c + h == x) & (c == cc)

                @pl.when(jnp.logical_not(own))
                def _():
                    send(ct.at[cc, h, sl], ct.at[cc, h, sl], sq.at[p, 0], rq.at[p, cc, h], sib).wait_recv()

    rows = br.shape[0]
    brow = lax.rem(dp, 16)
    src_b = bv.at[brow // 4, pl.ds(pl.multiple_of(lax.rem(brow, 4) * rows, rows), rows), :]
    cbs = [send(src_b, br, sb.at[d - 1], rb, dev(xd[d], y, z, c)) for d in range(1, NX)]

    def basis_send():
        @pl.when(x == y)
        def _():
            for cp in cbs:
                cp.start()

    def basis_columns():
        @pl.when(x == y)
        def _():
            loc = pltpu.make_async_copy(src_b, br, rb)
            loc.start()
            loc.wait()

        @pl.when(x != y)
        def _():
            cbs[0].wait_recv()

        ri = lax.broadcasted_iota(jnp.int32, (512, 512), 0)
        ji = lax.broadcasted_iota(jnp.int32, (512, 512), 1)
        jl = lax.broadcasted_iota(jnp.int32, (rows, 512), 1)
        for cc in range(2):
            e = (ri == (ji & ~8) + cc * 8).astype(F32).astype(BF16)
            t = jnp.dot(br[...], e, preferred_element_type=F32)
            for s in range(2):
                be[s, :, cc * 512:(cc + 1) * 512] = jnp.where(((jl >> 3) & 1) == s, t, 0.0).astype(BF16)

    def y_copies(k):
        w = pl.ds(0, WIDTHS[k])
        up, dn = dev(x, yd[1], z, c), dev(x, yd[3], z, c)
        to = (up, up, dn) if k % 2 == 0 else (dn, dn, up)
        return [send(ys.at[k, i, :, w], yr.at[k, i, :, w], sy.at[k, i], ry.at[k, i], to[i]) for i in range(3)]

    def z_copies(k):
        w = WIDTHS[k] // 2
        return [
            send(zs.at[k, zd[d], :, pl.ds(0, w)], zr.at[k, d - 1, :, pl.ds(0, w)], sz.at[k, d - 1], rz.at[k, d - 1], dev(x, y, zd[d], c))
            for d in range(1, NZ)
        ]

    def gz_copies(k):
        w = WIDTHS[k] // 2
        mine = db.at[k, c, y, z, :, pl.ds(0, w)]
        out = [send(mine, mine, sg.at[k, d - 1], rg.at[k, d - 1], dev(x, y, zd[d], c)) for d in range(1, NZ)]
        inn = []
        for d in range(1, NZ):
            zz = lax.rem(z + NZ - d, NZ)
            theirs = db.at[k, c, y, zz, :, pl.ds(0, w)]
            inn.append(send(theirs, theirs, sg.at[k, d - 1], rg.at[k, d - 1], dev(x, y, zz, c)))
        return out, inn

    def gy_copies(k):
        w = WIDTHS[k] // 2
        blk = lambda yy: db.at[k, c, yy, :, :, pl.ds(0, w)]
        lo = lambda yy: db.at[k, c, yy, pl.ds(0, 4), :, pl.ds(0, w)]
        hi = lambda yy: db.at[k, c, yy, pl.ds(4, 4), :, pl.ds(0, w)]
        up, dn = dev(x, yd[1], z, c), dev(x, yd[3], z, c)
        first = [
            send(blk(y), blk(y), sh.at[k, 0], rh.at[k, 0], up),
            send(blk(y), blk(y), sh.at[k, 1], rh.at[k, 1], dn),
        ]
        first_in = [
            send(blk(yd[3]), blk(yd[3]), sh.at[k, 0], rh.at[k, 0], up),
            send(blk(yd[1]), blk(yd[1]), sh.at[k, 1], rh.at[k, 1], dn),
        ]
        second = [
            send(lo(yd[3]), lo(yd[3]), sh.at[k, 2], rh.at[k, 2], up),
            send(hi(yd[1]), hi(yd[1]), sh.at[k, 3], rh.at[k, 3], dn),
        ]
        second_in = [
            send(lo(yd[2]), lo(yd[2]), sh.at[k, 2], rh.at[k, 2], up),
            send(hi(yd[2]), hi(yd[2]), sh.at[k, 3], rh.at[k, 3], dn),
        ]
        return first, first_in, second, second_in

    def k_copies(k):
        w = WIDTHS[k] // 2
        blk = lambda cc, yy: db.at[k, cc, yy, :, :, pl.ds(0, w)]
        out = [send(blk(c, yd[d]), blk(c, yd[d]), sk.at[k, d], rk.at[k, d], sib) for d in range(NY)]
        inn = [send(blk(oc, yd[d]), blk(oc, yd[d]), sk.at[k, d], rk.at[k, d], sib) for d in range(NY)]
        return out, inn

    def low(j0, j1, k):
        s0, w = STARTS[k], WIDTHS[k]
        n = (j1 - j0) * 32
        parts = []
        for h in range(2):
            l = jnp.dot(ct[0, h, j0:j1].reshape(n, -1), u[0, :, s0:s0 + w], preferred_element_type=F32)
            l += jnp.dot(ct[1, h, j0:j1].reshape(n, -1), u[1, :, s0:s0 + w], preferred_element_type=F32)
            parts.append(l)
        return [jnp.concatenate([q[i * 32:(i + 1) * 32] for q in parts], axis=0) for i in range(j1 - j0)]

    def s0(k):
        w = WIDTHS[k]
        ys[k, 0, :, 0:w] = low(0, 1, k)[0].astype(BF16)
        y_copies(k)[0].start()

    def s1(k):
        s0, w = STARTS[k], WIDTHS[k]
        up, dn, own = low(1, 4, k)
        relayed, direct = (up, dn) if k % 2 == 0 else (dn, up)
        lf[:, s0:s0 + w] = own
        cps = y_copies(k)
        ys[k, 2, :, 0:w] = direct.astype(BF16)
        cps[2].start()
        cps[0].wait_recv()
        ys[k, 1, :, 0:w] = (relayed + yr[k, 0, :, 0:w].astype(F32)).astype(BF16)
        cps[1].start()

    def s2(k):
        s0, w = STARTS[k], WIDTHS[k]
        g = lf[:, s0:s0 + w]
        for i in (2, 1):
            y_copies(k)[i].wait_recv()
            g = g + yr[k, i, :, 0:w].astype(F32)
        for zz in range(NZ):
            part = g[zz * 8:(zz + 1) * 8]
            zf[zz, :, s0:s0 + w] = part
            zs[k, zz, :, 0:w // 2] = jnp.concatenate([part[:, :w // 2], part[:, w // 2:]], axis=0).astype(BF16)
        for cp in z_copies(k):
            cp.start()

    def s3(k):
        s0, w = STARTS[k], WIDTHS[k]
        for cp in z_copies(k):
            cp.wait_recv()
        t = zr[k, 0, :, 0:w // 2].astype(F32)
        for d in range(1, NZ - 1):
            t = t + zr[k, d, :, 0:w // 2].astype(F32)
        g = zf[z, :, s0:s0 + w] + jnp.concatenate([t[0:8], t[8:16]], axis=1)
        a, b, dr = adam_rows(mv[:, s0:s0 + w], vv[:, s0:s0 + w], g)
        nm[:, s0:s0 + w] = a
        nv[:, s0:s0 + w] = b
        db[k, c, y, z, :, 0:w // 2] = jnp.concatenate([dr[:, :w // 2], dr[:, w // 2:]], axis=0).astype(BF16)
        for cp in gz_copies(k)[0]:
            cp.start()

    def s4(k):
        for cp in gz_copies(k)[1]:
            cp.wait_recv()
        for cp in gy_copies(k)[0]:
            cp.start()
        k_copies(k)[0][0].start()

    def s5(k):
        _, first_in, second, _ = gy_copies(k)
        out = k_copies(k)[0]
        first_in[0].wait_recv()
        second[0].start()
        first_in[1].wait_recv()
        second[1].start()
        out[3].start()
        out[1].start()

    def s6(k):
        for cp in gy_copies(k)[3]:
            cp.wait_recv()
        k_copies(k)[0][2].start()

    def s7(k):
        s0, w = STARTS[k], WIDTHS[k]
        for cp in k_copies(k)[1]:
            cp.wait_recv()
        d_all = db[k, :, :, :, :, 0:w // 2].reshape(1024, w // 2)
        for s in range(2):
            o = s0 + s * (w // 2)
            wo[:, o:o + w // 2] = 0.25 * jnp.dot(be[s], d_all, preferred_element_type=F32)

    x_reduce(0)
    x_reduce(1)
    lu.wait()
    cu_in.wait_recv()
    x_gathered(0)
    for k in range(NCH):
        s0(k)
    x_gathered(1)
    lm.wait()
    lv.wait()
    basis_send()

    stages = [s1, s2, s3, s4, s5, s6, s7]
    order = []
    for k in range(NCH):
        t = PACE * k
        for i in range(len(stages)):
            order.append((t, -i, k))
            t += LATENCY[i]
    for n, (_, i, k) in enumerate(sorted(order)):
        stages[-i](k)
        if i == -1 and k == NCH - 1:
            basis_columns()

    for p in range(2):
        for cp in cx[p]:
            cp.wait_send()
        for d in range(1, NX):
            q_copies(p)[d].wait_send()

        @pl.when(cq != c)
        def _():
            q_copies(p)[0].wait_send()

    cu.wait_send()

    @pl.when(x == y)
    def _():
        for cp in cbs:
            cp.wait_send()

    for k in range(NCH):
        first, _, second, _ = gy_copies(k)
        for cp in y_copies(k) + z_copies(k) + gz_copies(k)[0] + first + second + k_copies(k)[0]:
            cp.wait_send()


def body(features, up_cotangent, proj_basis, first_moment, second_moment):
    tok, feat = features.shape
    depth, rank = proj_basis.shape
    cols = up_cotangent.shape[1]
    kw = feat // KB
    rows = 128
    dma = pltpu.SemaphoreType.DMA
    anyspec = pl.BlockSpec(memory_space=pl.ANY)
    wu, nf, ns = pl.pallas_call(
        kernel,
        out_shape=(
            pltpu.VMEM((rows, cols), F32),
            pltpu.VMEM(first_moment.shape, F32),
            pltpu.VMEM(second_moment.shape, F32),
        ),
        in_specs=[anyspec] * 5,
        out_specs=(pl.BlockSpec(memory_space=pltpu.VMEM),) * 3,
        scratch_shapes=[
            pltpu.VMEM((KB, tok, kw), BF16),
            pltpu.VMEM((KB, kw, rank), BF16),
            pltpu.VMEM((2, tok, cols), BF16),
            pltpu.VMEM((8, cols), F32),
            pltpu.VMEM((8, cols), F32),
            pltpu.VMEM((tok, rank), F32),
            pltpu.VMEM((NX, NY, 32, tok), F32),
            pltpu.VMEM((NX, NY, 32, tok), BF16),
            pltpu.VMEM((NX - 1, NY, 32, tok), BF16),
            pltpu.VMEM((NY, 32, tok), BF16),
            pltpu.VMEM((2, 2, NY, 32, tok), BF16),
            pltpu.VMEM((64, cols), F32),
            pltpu.VMEM((NCH, 3, 64, WMAX), BF16),
            pltpu.VMEM((NCH, 3, 64, WMAX), BF16),
            pltpu.VMEM((NZ, 8, cols), F32),
            pltpu.VMEM((NCH, NZ, 16, WMAX // 2), BF16),
            pltpu.VMEM((NCH, NZ - 1, 16, WMAX // 2), BF16),
            pltpu.VMEM((NCH, 2, NY, NZ, 16, WMAX // 2), BF16),
            pltpu.VMEM((rows, rank), BF16),
            pltpu.VMEM((2, rows, 2 * rank), BF16),
            dma((KB,)), dma((KB,)), dma(()), dma((2,)),
            dma((2, 3)), dma((2, 3)), dma((2, 4)), dma((2, 2, 2)), dma(()), dma(()), dma((3,)), dma(()),
            dma((NCH, 3)), dma((NCH, 3)), dma((NCH, 7)), dma((NCH, 7)), dma((NCH, 7)), dma((NCH, 7)),
            dma((NCH, 4)), dma((NCH, 4)), dma((NCH, 4)), dma((NCH, 4)),
        ],
        compiler_params=pltpu.CompilerParams(
            collective_id=0, has_side_effects=True, vmem_limit_bytes=56 * 2**20
        ),
        cost_estimate=pl.CostEstimate(flops=4 * 10**9, bytes_accessed=12 * 10**6, transcendentals=0),
        name="galore",
    )(features, up_cotangent, proj_basis, first_moment, second_moment)
    return (wu, nf, ns)


def solution(mesh):
    return jax.shard_map(
        body,
        mesh=mesh,
        in_specs=(P("dp", "mp"), P("dp", "mp"), P("mp", None), P("dp", "mp"), P("dp", "mp")),
        out_specs=(P("dp", "mp"), P("dp", "mp"), P("dp", "mp")),
        check_vma=False,
    )
```

```python
import jax
import jax.numpy as jnp
from jax import lax
from jax.experimental import pallas as pl
from jax.experimental.pallas import tpu as pltpu
from jax.sharding import PartitionSpec as P

STEP = 10
P_START, P_PACE, Q_PACE, BASIS_AT = 0.1, 0.8, 5.0, 12.0
P1, P2, P3, P4, P5, P6 = 3.5, 5.5, 5.5, 4.0, 4.0, 2.0
Q1, Q2, Q3, Q4, Q5 = 9.0, 3.5, 3.5, 9.0, 2.0
PARTS = (pl.ds(0, 1), pl.ds(1, 3))
NX, NY, NZ = 4, 4, 8
COLS = 3584
WIDTHS = (512, 512, 512, 512, 512, 512, 512)
STARTS = tuple(sum(WIDTHS[:i]) for i in range(len(WIDTHS)))
NCH = len(WIDTHS)
WMAX = max(WIDTHS)
NQ = 1
KB = 4
F32, BF16 = jnp.float32, jnp.bfloat16


def adam_rows(first_moment, second_moment, low_grad):
    new_first = 0.9 * first_moment + 0.1 * low_grad
    new_second = 0.999 * second_moment + 0.001 * low_grad * low_grad
    first_hat = new_first / (1.0 - 0.9**STEP)
    second_hat = new_second / (1.0 - 0.999**STEP)
    direction = first_hat / (jnp.sqrt(second_hat) + 1e-08)
    return (new_first, new_second, direction)


def kernel(
    f_hbm, u_hbm, b_hbm, m_hbm, v_hbm,
    wo, nm, nv,
    fv, bv, u, mv, vv,
    acc, pt, xs, xr, qv, ct, qs, qr, qf, qys, qyr,
    lf, ys, yr, zf, zs, zr, db, br, be,
    ld_f, ld_b, ld_u, ld_m,
    sx, rx, sq, rq, su, ru, sb, rb,
    sy, ry, sz, rz, sg, rg, sh, rh, sk, rk,
    sqz, rqz, sqy, rqy, sqg, rqg, sqh, rqh,
):
    dp = lax.axis_index("dp")
    x = lax.axis_index("mp")
    c = lax.rem(dp, 2)
    z = lax.rem(dp // 2, NZ)
    y = dp // (2 * NZ)
    oc = 1 - c

    def dev(x_, y_, z_, c_):
        return ((y_ * NZ + z_) * 2 + c_, x_)

    def send(src, dst, ss, rs, to):
        return pltpu.make_async_remote_copy(
            src_ref=src, dst_ref=dst, send_sem=ss, recv_sem=rs,
            device_id=to, device_id_type=pl.DeviceIdType.MESH,
        )

    xd = [lax.rem(x + d, NX) for d in range(NX)]
    yd = [lax.rem(y + d, NY) for d in range(NY)]
    zd = [lax.rem(z + d, NZ) for d in range(NZ)]
    yo = [yd[2], yd[1], yd[3], yd[0]]
    sib = dev(x, y, z, oc)

    kw = fv.shape[2]
    lf_c = [pltpu.make_async_copy(f_hbm.at[:, pl.ds(k * kw, kw)], fv.at[k], ld_f.at[k]) for k in range(KB)]
    lb_c = [pltpu.make_async_copy(b_hbm.at[pl.ds(k * kw, kw), :], bv.at[k], ld_b.at[k]) for k in range(KB)]
    for k in range(KB):
        lb_c[k].start()
        lf_c[k].start()
    lu = pltpu.make_async_copy(u_hbm, u.at[c], ld_u)
    lu.start()
    lm = pltpu.make_async_copy(m_hbm, mv, ld_m.at[0])
    lv = pltpu.make_async_copy(v_hbm, vv, ld_m.at[1])
    lm.start()
    lv.start()

    bar = pltpu.get_barrier_semaphore()
    peers = [sib]
    for d in range(1, NX):
        peers += [dev(xd[d], y, z, c), dev(xd[d], y, z, oc)]
    peers += [dev(x, yd[d], z, c) for d in range(1, NY)]
    peers += [dev(x, y, zd[d], c) for d in range(1, NZ)]
    for p in peers:
        pl.semaphore_signal(bar, inc=1, device_id=p, device_id_type=pl.DeviceIdType.MESH)

    for k in range(KB):
        lb_c[k].wait()
        lf_c[k].wait()
        part = jnp.dot(fv[k], bv[k], preferred_element_type=F32)
        if k == 0:
            acc[...] = part
        else:
            acc[...] += part
    for yy in range(NY):
        tt = acc[:, yy * 128:(yy + 1) * 128].T
        for h in range(2):
            for zl in range(4):
                for cc in range(2):
                    r = ((h * 4 + zl) * 2 + cc) * 8
                    pt[2 * cc + h, yy, zl * 8:zl * 8 + 8, :] = tt[r:r + 8, :]
    for j in range(NY):
        for xx in range(NX):
            xs[xx, j] = pt[xx, yo[j]].astype(BF16)

    pl.semaphore_wait(bar, len(peers))
    cx = [
        [
            send(xs.at[xd[d], sl], xr.at[d - 1, sl], sx.at[p, d - 1], rx.at[p, d - 1], dev(xd[d], y, z, c))
            for d in range(1, NX)
        ]
        for p, sl in enumerate(PARTS)
    ]
    for p in range(2):
        for cp in cx[p]:
            cp.start()
    cu = send(u_hbm, u.at[c], su, ru, sib)
    cu.start()
    cu_in = send(u_hbm, u.at[oc], su, ru, sib)

    hx = lax.rem(x, 2)
    cq = x // 2

    def q_copies(p):
        sl = PARTS[p]
        return [send(qv.at[sl], ct.at[c, hx, sl], sq.at[p, d], rq.at[p, c, hx], dev(xd[d], y, z, cq)) for d in range(NX)]

    def x_reduce(p):
        for cp in cx[p]:
            cp.wait_recv()
        for j in (0,) if p == 0 else (1, 2, 3):
            q = pt[x, yo[j]]
            for d in range(NX - 1):
                q = q + xr[d, j].astype(F32)
            qv[j] = q.astype(BF16)
        cps = q_copies(p)
        for d in range(1, NX):
            cps[d].start()

        @pl.when(cq != c)
        def _():
            cps[0].start()

        @pl.when(cq == c)
        def _():
            for j in (0,) if p == 0 else (1, 2, 3):
                ct[c, hx, j] = qv[j]

    def x_gathered(p):
        sl = PARTS[p]
        for cc in range(2):
            for h in range(2):
                own = (2 * c + h == x) & (c == cc)

                @pl.when(jnp.logical_not(own))
                def _():
                    send(ct.at[cc, h, sl], ct.at[cc, h, sl], sq.at[p, 0], rq.at[p, cc, h], sib).wait_recv()

    rows = br.shape[0]
    brow = lax.rem(dp, 16)
    src_b = bv.at[brow // 4, pl.ds(pl.multiple_of(lax.rem(brow, 4) * rows, rows), rows), :]
    cbs = [send(src_b, br, sb.at[d - 1], rb, dev(xd[d], y, z, c)) for d in range(1, NX)]

    def basis_send():
        @pl.when(x == y)
        def _():
            for cp in cbs:
                cp.start()

    def basis_columns():
        @pl.when(x == y)
        def _():
            loc = pltpu.make_async_copy(src_b, br, rb)
            loc.start()
            loc.wait()

        @pl.when(x != y)
        def _():
            cbs[0].wait_recv()

        ri = lax.broadcasted_iota(jnp.int32, (512, 512), 0)
        ji = lax.broadcasted_iota(jnp.int32, (512, 512), 1)
        jl = lax.broadcasted_iota(jnp.int32, (rows, 512), 1)
        for cc in range(2):
            e = (ri == (ji & ~8) + cc * 8).astype(F32).astype(BF16)
            t = jnp.dot(br[...], e, preferred_element_type=F32)
            for s in range(2):
                be[s, :, cc * 512:(cc + 1) * 512] = jnp.where(((jl >> 3) & 1) == s, t, 0.0).astype(BF16)

    def y_copies(k):
        w = pl.ds(0, WIDTHS[k])
        up, dn = dev(x, yd[1], z, c), dev(x, yd[3], z, c)
        to = (up, up, dn) if k % 2 == 0 else (dn, dn, up)
        return [send(ys.at[k, i, :, w], yr.at[k, i, :, w], sy, ry.at[k, i], to[i]) for i in range(3)]

    def z_copies(k):
        w = WIDTHS[k] // 2
        return [
            send(zs.at[k, zd[d], :, pl.ds(0, w)], zr.at[k, d - 1, :, pl.ds(0, w)], sz, rz.at[k], dev(x, y, zd[d], c))
            for d in range(1, NZ)
        ]

    def gz_copies(k):
        w = WIDTHS[k] // 2
        mine = db.at[k, c, y, z, :, pl.ds(0, w)]
        out = [send(mine, mine, sg, rg.at[k], dev(x, y, zd[d], c)) for d in range(1, NZ)]
        return out

    def gy_copies(k):
        w = WIDTHS[k] // 2
        blk = lambda yy: db.at[k, c, yy, :, :, pl.ds(0, w)]
        lo = lambda yy: db.at[k, c, yy, pl.ds(0, 4), :, pl.ds(0, w)]
        hi = lambda yy: db.at[k, c, yy, pl.ds(4, 4), :, pl.ds(0, w)]
        up, dn = dev(x, yd[1], z, c), dev(x, yd[3], z, c)
        first = [
            send(blk(y), blk(y), sh, rh.at[k, 0], up),
            send(blk(y), blk(y), sh, rh.at[k, 1], dn),
        ]
        first_in = [
            send(blk(yd[3]), blk(yd[3]), sh, rh.at[k, 0], up),
            send(blk(yd[1]), blk(yd[1]), sh, rh.at[k, 1], dn),
        ]
        second = [
            send(lo(yd[3]), lo(yd[3]), sh, rh.at[k, 2], up),
            send(hi(yd[1]), hi(yd[1]), sh, rh.at[k, 2], dn),
        ]
        return first, first_in, second

    def k_copies(k):
        w = WIDTHS[k] // 2
        blk = lambda cc, yy: db.at[k, cc, yy, :, :, pl.ds(0, w)]
        return [send(blk(c, yd[d]), blk(c, yd[d]), sk, rk.at[k], sib) for d in range(NY)]

    def low(j0, j1, k):
        s0, w = STARTS[k], WIDTHS[k]
        n = (j1 - j0) * 32
        parts = []
        for h in range(2):
            l = jnp.dot(ct[0, h, j0:j1].reshape(n, -1), u[0, :, s0:s0 + w], preferred_element_type=F32)
            l += jnp.dot(ct[1, h, j0:j1].reshape(n, -1), u[1, :, s0:s0 + w], preferred_element_type=F32)
            parts.append(l)
        return [jnp.concatenate([q[i * 32:(i + 1) * 32] for q in parts], axis=0) for i in range(j1 - j0)]

    def s0(k):
        w = WIDTHS[k]
        ys[k, 0, :, 0:w] = low(0, 1, k)[0].astype(BF16)
        y_copies(k)[0].start()

    def s1(k):
        s0, w = STARTS[k], WIDTHS[k]
        up, dn, own = low(1, 4, k)
        relayed, direct = (up, dn) if k % 2 == 0 else (dn, up)
        lf[:, s0:s0 + w] = own
        cps = y_copies(k)
        ys[k, 2, :, 0:w] = direct.astype(BF16)
        cps[2].start()
        cps[0].wait_recv()
        ys[k, 1, :, 0:w] = (relayed + yr[k, 0, :, 0:w].astype(F32)).astype(BF16)
        cps[1].start()

    def s2(k):
        s0, w = STARTS[k], WIDTHS[k]
        g = lf[:, s0:s0 + w]
        for i in (2, 1):
            y_copies(k)[i].wait_recv()
            g = g + yr[k, i, :, 0:w].astype(F32)
        for zz in range(NZ):
            part = g[zz * 8:(zz + 1) * 8]
            zf[zz, :, s0:s0 + w] = part
            zs[k, zz, :, 0:w // 2] = jnp.concatenate([part[:, :w // 2], part[:, w // 2:]], axis=0).astype(BF16)
        for cp in z_copies(k):
            cp.start()

    def step(k, g):
        s0, w = STARTS[k], WIDTHS[k]
        a, b, dr = adam_rows(mv[:, s0:s0 + w], vv[:, s0:s0 + w], g)
        nm[:, s0:s0 + w] = a
        nv[:, s0:s0 + w] = b
        db[k, c, y, z, :, 0:w // 2] = jnp.concatenate([dr[:, :w // 2], dr[:, w // 2:]], axis=0).astype(BF16)

    def s3(k):
        s0, w = STARTS[k], WIDTHS[k]
        got(zr.at[k], rz.at[k])
        t = zr[k, 0, :, 0:w // 2].astype(F32)
        for d in range(1, NZ - 1):
            t = t + zr[k, d, :, 0:w // 2].astype(F32)
        step(k, zf[z, :, s0:s0 + w] + jnp.concatenate([t[0:8], t[8:16]], axis=1))
        for cp in gz_copies(k):
            cp.start()

    def s4(k):
        got(zr.at[k], rg.at[k])
        for cp in gy_copies(k)[0]:
            cp.start()
        k_copies(k)[0].start()

    def s5(k):
        _, first_in, second = gy_copies(k)
        out = k_copies(k)
        first_in[0].wait_recv()
        second[0].start()
        first_in[1].wait_recv()
        second[1].start()
        out[3].start()
        out[1].start()

    def s6(k):
        got(db.at[k, c, 0], rh.at[k, 2])
        k_copies(k)[2].start()

    def qz_copies(k):
        w = pl.ds(0, WIDTHS[k])
        return [
            send(qs.at[k, zd[d], :, w], qr.at[k, d - 1, :, w], sqz, rqz.at[k], dev(x, y, zd[d], c))
            for d in range(1, NZ)
        ]

    def qy_copies(k):
        w = pl.ds(0, WIDTHS[k] // 2)
        return [
            send(qys.at[k, j, :, w], qyr.at[k, j, :, w], sqy, rqy.at[k], dev(x, yo[j], z, c))
            for j in range(3)
        ]

    def qg_copies(k):
        mine = db.at[k, c, y, z, :, pl.ds(0, WIDTHS[k] // 2)]
        return [send(mine, mine, sqg, rqg.at[k], dev(x, yd[d], z, c)) for d in range(1, NY)]

    def qh_copies(k):
        mine = db.at[k, c, :, z, :, pl.ds(0, WIDTHS[k] // 2)]
        return [send(mine, mine, sqh, rqh.at[k], dev(x, y, zd[d], c)) for d in range(1, NZ)]

    def got(ref, sem):
        send(ref, ref, sem, sem, sib).wait_recv()

    def left(ref, sem):
        send(ref, ref, sem, sem, sib).wait_send()

    def q1(k):
        s0, w = STARTS[k], WIDTHS[k]
        for h in range(2):
            l = jnp.dot(ct[0, h].reshape(128, -1), u[0, :, s0:s0 + w], preferred_element_type=F32)
            l += jnp.dot(ct[1, h].reshape(128, -1), u[1, :, s0:s0 + w], preferred_element_type=F32)
            for zl in range(4):
                part = jnp.concatenate([l[j * 32 + zl * 8:j * 32 + zl * 8 + 8] for j in range(NY)], axis=0)
                qf[k, h * 4 + zl, :, 0:w] = part
                qs[k, h * 4 + zl, :, 0:w] = part.astype(BF16)
        for cp in qz_copies(k):
            cp.start()

    def halves(part):
        w = part.shape[1] // 2
        return jnp.concatenate([part[:, :w], part[:, w:]], axis=0).astype(BF16)

    def q2(k):
        w = WIDTHS[k]
        got(qr.at[k], rqz.at[k])
        g = qf[k, z, :, 0:w]
        for d in range(NZ - 1):
            g = g + qr[k, d, :, 0:w].astype(F32)
        qf[k, 0, 0:8, 0:w] = g[24:32]
        for j in range(3):
            qys[k, j, :, 0:w // 2] = halves(g[j * 8:j * 8 + 8])
        for cp in qy_copies(k):
            cp.start()

    def q3(k):
        w = WIDTHS[k]
        got(qyr.at[k], rqy.at[k])
        t = qyr[k, 0, :, 0:w // 2].astype(F32)
        for j in range(1, 3):
            t = t + qyr[k, j, :, 0:w // 2].astype(F32)
        step(k, qf[k, 0, 0:8, 0:w] + jnp.concatenate([t[0:8], t[8:16]], axis=1))
        for cp in qg_copies(k):
            cp.start()

    def q4(k):
        got(qyr.at[k], rqg.at[k])
        for cp in qh_copies(k):
            cp.start()

    def q5(k):
        got(zr.at[pl.ds(0, NY)], rqh.at[k])
        for cp in k_copies(k):
            cp.start()

    def s7(k):
        s0, w = STARTS[k], WIDTHS[k]
        got(db.at[k, oc], rk.at[k])
        d_all = db[k, :, :, :, :, 0:w // 2].reshape(1024, w // 2)
        for s in range(2):
            o = s0 + s * (w // 2)
            wo[:, o:o + w // 2] = 0.25 * jnp.dot(be[s], d_all, preferred_element_type=F32)

    x_reduce(0)
    x_reduce(1)
    lu.wait()
    cu_in.wait_recv()
    x_gathered(0)
    for k in range(NQ, NCH):
        s0(k)
    x_gathered(1)
    lm.wait()
    lv.wait()
    basis_send()

    p_stages = ((s1, P1), (s2, P2), (s3, P3), (s4, P4), (s5, P5), (s6, P6), (s7, 0.0))
    q_stages = ((q1, Q1), (q2, Q2), (q3, Q3), (q4, Q4), (q5, Q5), (s7, 0.0))
    order = [(BASIS_AT, 0, 0, lambda k: basis_columns())]
    for k in range(NCH):
        t = Q_PACE * k if k < NQ else P_PACE * (k - NQ) + P_START
        for i, (stage, latency) in enumerate(q_stages if k < NQ else p_stages):
            order.append((t, -i, k, stage))
            t += latency
    for _, _, k, stage in sorted(order, key=lambda e: e[:3]):
        stage(k)

    for p in range(2):
        for cp in cx[p]:
            cp.wait_send()
        for d in range(1, NX):
            q_copies(p)[d].wait_send()

        @pl.when(cq != c)
        def _():
            q_copies(p)[0].wait_send()

    cu.wait_send()

    @pl.when(x == y)
    def _():
        for cp in cbs:
            cp.wait_send()

    rest = pl.ds(NQ, NCH - NQ)
    left(ys.at[rest], sy)
    left(zr.at[rest], sz)
    left(zr.at[rest], sg)
    left(db.at[rest, 0, pl.ds(0, 3)], sh)
    left(db.at[:, 0], sk)
    left(qr, sqz)
    left(qyr, sqy)
    left(qyr, sqg)
    for k in range(NQ):
        left(zr.at[pl.ds(0, NY)], sqh)


def body(features, up_cotangent, proj_basis, first_moment, second_moment):
    tok, feat = features.shape
    depth, rank = proj_basis.shape
    cols = up_cotangent.shape[1]
    kw = feat // KB
    rows = 128
    dma = pltpu.SemaphoreType.DMA
    anyspec = pl.BlockSpec(memory_space=pl.ANY)
    wu, nf, ns = pl.pallas_call(
        kernel,
        out_shape=(
            pltpu.VMEM((rows, cols), F32),
            pltpu.VMEM(first_moment.shape, F32),
            pltpu.VMEM(second_moment.shape, F32),
        ),
        in_specs=[anyspec] * 5,
        out_specs=(pl.BlockSpec(memory_space=pltpu.VMEM),) * 3,
        scratch_shapes=[
            pltpu.VMEM((KB, tok, kw), BF16),
            pltpu.VMEM((KB, kw, rank), BF16),
            pltpu.VMEM((2, tok, cols), BF16),
            pltpu.VMEM((8, cols), F32),
            pltpu.VMEM((8, cols), F32),
            pltpu.VMEM((tok, rank), F32),
            pltpu.VMEM((NX, NY, 32, tok), F32),
            pltpu.VMEM((NX, NY, 32, tok), BF16),
            pltpu.VMEM((NX - 1, NY, 32, tok), BF16),
            pltpu.VMEM((NY, 32, tok), BF16),
            pltpu.VMEM((2, 2, NY, 32, tok), BF16),
            pltpu.VMEM((NQ, NZ, 32, WMAX), BF16),
            pltpu.VMEM((NQ, NZ - 1, 32, WMAX), BF16),
            pltpu.VMEM((NQ, NZ, 32, WMAX), F32),
            pltpu.VMEM((NQ, 3, 16, WMAX // 2), BF16),
            pltpu.VMEM((NQ, 3, 16, WMAX // 2), BF16),
            pltpu.VMEM((64, cols), F32),
            pltpu.VMEM((NCH, 3, 64, WMAX), BF16),
            pltpu.VMEM((NCH, 3, 64, WMAX), BF16),
            pltpu.VMEM((NZ, 8, cols), F32),
            pltpu.VMEM((NCH, NZ, 16, WMAX // 2), BF16),
            pltpu.VMEM((NCH, NZ - 1, 16, WMAX // 2), BF16),
            pltpu.VMEM((NCH, 2, NY, NZ, 16, WMAX // 2), BF16),
            pltpu.VMEM((rows, rank), BF16),
            pltpu.VMEM((2, rows, 2 * rank), BF16),
            dma((KB,)), dma((KB,)), dma(()), dma((2,)),
            dma((2, 3)), dma((2, 3)), dma((2, 4)), dma((2, 2, 2)), dma(()), dma(()), dma((3,)), dma(()),
            dma(()), dma((NCH, 3)), dma(()), dma((NCH,)), dma(()), dma((NCH,)),
            dma(()), dma((NCH, 3)), dma(()), dma((NCH,)),
            dma(()), dma((NQ,)), dma(()), dma((NQ,)), dma(()), dma((NQ,)), dma(()), dma((NQ,)),
        ],
        compiler_params=pltpu.CompilerParams(
            collective_id=0, has_side_effects=True, vmem_limit_bytes=56 * 2**20
        ),
        cost_estimate=pl.CostEstimate(flops=4 * 10**9, bytes_accessed=12 * 10**6, transcendentals=0),
        name="galore",
    )(features, up_cotangent, proj_basis, first_moment, second_moment)
    return (wu, nf, ns)


def solution(mesh):
    return jax.shard_map(
        body,
        mesh=mesh,
        in_specs=(P("dp", "mp"), P("dp", "mp"), P("mp", None), P("dp", "mp"), P("dp", "mp")),
        out_specs=(P("dp", "mp"), P("dp", "mp"), P("dp", "mp")),
        check_vma=False,
    )
```

```python
import jax
import jax.numpy as jnp
from jax import lax
from jax.experimental import pallas as pl
from jax.experimental.pallas import tpu as pltpu
from jax.sharding import PartitionSpec as P

STEP = 10
P_START, P_PACE, Q_PACE, BASIS_AT = 0.1, 0.8, 5.0, 20.0
P1, P2, P3, P4, P5, P6 = 3.5, 5.5, 5.5, 4.0, 4.0, 2.0
Q1, Q2, Q3, Q4, Q5 = 9.0, 3.5, 3.5, 9.0, 2.0
PARTS = (pl.ds(0, 1), pl.ds(1, 3))
NX, NY, NZ = 4, 4, 8
COLS = 3584
WIDTHS = (512, 512, 512, 512, 512, 512, 512)
STARTS = tuple(sum(WIDTHS[:i]) for i in range(len(WIDTHS)))
NCH = len(WIDTHS)
WMAX = max(WIDTHS)
NQ = 1
KB = 4
F32, BF16 = jnp.float32, jnp.bfloat16


def adam_rows(first_moment, second_moment, low_grad):
    new_first = 0.9 * first_moment + 0.1 * low_grad
    new_second = 0.999 * second_moment + 0.001 * low_grad * low_grad
    first_hat = new_first / (1.0 - 0.9**STEP)
    second_hat = new_second / (1.0 - 0.999**STEP)
    direction = first_hat / (jnp.sqrt(second_hat) + 1e-08)
    return (new_first, new_second, direction)


def kernel(
    f_hbm, u_hbm, b_hbm, m_hbm, v_hbm,
    wo, nm, nv,
    fv, bv, u, mv, vv,
    acc, pt, xs, xr, qv, ct, qs, qr, qf, qys, qyr,
    lf, ys, yr, zf, zs, zr, db, br, be,
    ld_f, ld_b, ld_u, ld_m,
    sx, rx, sq, rq, su, ru, sb, rb,
    sy, ry, sz, rz, sg, rg, sh, rh, sk, rk,
    sqz, rqz, sqy, rqy, sqg, rqg, sqh, rqh,
):
    dp = lax.axis_index("dp")
    x = lax.axis_index("mp")
    c = lax.rem(dp, 2)
    z = lax.rem(dp // 2, NZ)
    y = dp // (2 * NZ)
    oc = 1 - c

    def dev(x_, y_, z_, c_):
        return ((y_ * NZ + z_) * 2 + c_, x_)

    def send(src, dst, ss, rs, to):
        return pltpu.make_async_remote_copy(
            src_ref=src, dst_ref=dst, send_sem=ss, recv_sem=rs,
            device_id=to, device_id_type=pl.DeviceIdType.MESH,
        )

    xd = [lax.rem(x + d, NX) for d in range(NX)]
    yd = [lax.rem(y + d, NY) for d in range(NY)]
    zd = [lax.rem(z + d, NZ) for d in range(NZ)]
    yo = [yd[2], yd[1], yd[3], yd[0]]
    sib = dev(x, y, z, oc)
    ydev = [dev(x, yd[d], z, c) for d in range(NY)]
    zdev = [dev(x, y, zd[d], c) for d in range(NZ)]

    kw = fv.shape[2]
    lf_c = [pltpu.make_async_copy(f_hbm.at[:, pl.ds(k * kw, kw)], fv.at[k], ld_f.at[k]) for k in range(KB)]
    lb_c = [pltpu.make_async_copy(b_hbm.at[pl.ds(k * kw, kw), :], bv.at[k], ld_b.at[k]) for k in range(KB)]
    for k in range(KB):
        lb_c[k].start()
        lf_c[k].start()
    lu = pltpu.make_async_copy(u_hbm, u.at[c], ld_u)
    lu.start()
    lm = pltpu.make_async_copy(m_hbm, mv, ld_m.at[0])
    lv = pltpu.make_async_copy(v_hbm, vv, ld_m.at[1])
    lm.start()
    lv.start()

    bar = pltpu.get_barrier_semaphore()
    peers = [sib]
    for d in range(1, NX):
        peers += [dev(xd[d], y, z, c), dev(xd[d], y, z, oc)]
    peers += [dev(x, yd[d], z, c) for d in range(1, NY)]
    peers += [dev(x, y, zd[d], c) for d in range(1, NZ)]
    for p in peers:
        pl.semaphore_signal(bar, inc=1, device_id=p, device_id_type=pl.DeviceIdType.MESH)

    for k in range(KB):
        lb_c[k].wait()
        lf_c[k].wait()
        part = jnp.dot(fv[k], bv[k], preferred_element_type=F32)
        if k == 0:
            acc[...] = part
        else:
            acc[...] += part
    for yy in range(NY):
        tt = acc[:, yy * 128:(yy + 1) * 128].T
        for h in range(2):
            for zl in range(4):
                for cc in range(2):
                    r = ((h * 4 + zl) * 2 + cc) * 8
                    pt[2 * cc + h, yy, zl * 8:zl * 8 + 8, :] = tt[r:r + 8, :]
    for j in range(NY):
        for xx in range(NX):
            xs[xx, j] = pt[xx, yo[j]].astype(BF16)

    pl.semaphore_wait(bar, len(peers))
    cx = [
        [
            send(xs.at[xd[d], sl], xr.at[d - 1, sl], sx.at[p], rx.at[p], dev(xd[d], y, z, c))
            for d in range(1, NX)
        ]
        for p, sl in enumerate(PARTS)
    ]
    for p in range(2):
        for cp in cx[p]:
            cp.start()
    cu = send(u_hbm, u.at[c], su, ru, sib)
    cu.start()
    cu_in = send(u_hbm, u.at[oc], su, ru, sib)

    hx = lax.rem(x, 2)
    cq = x // 2

    def q_copies(p):
        sl = PARTS[p]
        return [send(qv.at[sl], ct.at[c, hx, sl], sq.at[p, d], rq.at[p, c, hx], dev(xd[d], y, z, cq)) for d in range(NX)]

    def x_reduce(p):
        got(xr.at[:, PARTS[p]], rx.at[p])
        for j in (0,) if p == 0 else (1, 2, 3):
            q = pt[x, yo[j]]
            for d in range(NX - 1):
                q = q + xr[d, j].astype(F32)
            qv[j] = q.astype(BF16)
        cps = q_copies(p)
        for d in range(1, NX):
            cps[d].start()

        @pl.when(cq != c)
        def _():
            cps[0].start()

        @pl.when(cq == c)
        def _():
            for j in (0,) if p == 0 else (1, 2, 3):
                ct[c, hx, j] = qv[j]

    def x_gathered(p):
        sl = PARTS[p]
        for cc in range(2):
            for h in range(2):
                own = (2 * c + h == x) & (c == cc)

                @pl.when(jnp.logical_not(own))
                def _():
                    send(ct.at[cc, h, sl], ct.at[cc, h, sl], sq.at[p, 0], rq.at[p, cc, h], sib).wait_recv()

    rows = br.shape[0]
    brow = lax.rem(dp, 16)
    src_b = bv.at[brow // 4, pl.ds(pl.multiple_of(lax.rem(brow, 4) * rows, rows), rows), :]
    cbs = [send(src_b, br, sb.at[d - 1], rb, dev(xd[d], y, z, c)) for d in range(1, NX)]

    def basis_send():
        @pl.when(x == y)
        def _():
            for cp in cbs:
                cp.start()

    def basis_columns():
        @pl.when(x == y)
        def _():
            loc = pltpu.make_async_copy(src_b, br, rb)
            loc.start()
            loc.wait()

        @pl.when(x != y)
        def _():
            cbs[0].wait_recv()

        ri = lax.broadcasted_iota(jnp.int32, (512, 512), 0)
        ji = lax.broadcasted_iota(jnp.int32, (512, 512), 1)
        jl = lax.broadcasted_iota(jnp.int32, (rows, 512), 1)
        for cc in range(2):
            e = (ri == (ji & ~8) + cc * 8).astype(F32).astype(BF16)
            t = jnp.dot(br[...], e, preferred_element_type=F32)
            for s in range(2):
                be[s, :, cc * 512:(cc + 1) * 512] = jnp.where(((jl >> 3) & 1) == s, t, 0.0).astype(BF16)

    def y_copies(k):
        w = pl.ds(0, WIDTHS[k])
        up, dn = ydev[1], ydev[3]
        to = (up, up, dn) if k % 2 == 0 else (dn, dn, up)
        return [send(ys.at[k, i, :, w], yr.at[k, i, :, w], sy, ry.at[k, i], to[i]) for i in range(3)]

    def z_copies(k):
        w = WIDTHS[k] // 2
        return [
            send(zs.at[k, zd[d], :, pl.ds(0, w)], zr.at[k, d - 1, :, pl.ds(0, w)], sz, rz.at[k], zdev[d])
            for d in range(1, NZ)
        ]

    def gz_copies(k):
        w = WIDTHS[k] // 2
        mine = db.at[k, c, y, z, :, pl.ds(0, w)]
        out = [send(mine, mine, sg, rg.at[k], zdev[d]) for d in range(1, NZ)]
        return out

    def gy_copies(k):
        w = WIDTHS[k] // 2
        blk = lambda yy: db.at[k, c, yy, :, :, pl.ds(0, w)]
        lo = lambda yy: db.at[k, c, yy, pl.ds(0, 4), :, pl.ds(0, w)]
        hi = lambda yy: db.at[k, c, yy, pl.ds(4, 4), :, pl.ds(0, w)]
        up, dn = ydev[1], ydev[3]
        first = [
            send(blk(y), blk(y), sh, rh.at[k, 0], up),
            send(blk(y), blk(y), sh, rh.at[k, 1], dn),
        ]
        first_in = [
            send(blk(yd[3]), blk(yd[3]), sh, rh.at[k, 0], up),
            send(blk(yd[1]), blk(yd[1]), sh, rh.at[k, 1], dn),
        ]
        second = [
            send(lo(yd[3]), lo(yd[3]), sh, rh.at[k, 2], up),
            send(hi(yd[1]), hi(yd[1]), sh, rh.at[k, 2], dn),
        ]
        return first, first_in, second

    def k_copies(k):
        w = WIDTHS[k] // 2
        blk = lambda cc, yy: db.at[k, cc, yy, :, :, pl.ds(0, w)]
        return [send(blk(c, yd[d]), blk(c, yd[d]), sk, rk.at[k], sib) for d in range(NY)]

    def low(j0, j1, k):
        s0, w = STARTS[k], WIDTHS[k]
        n = (j1 - j0) * 32
        parts = []
        for h in range(2):
            l = jnp.dot(ct[0, h, j0:j1].reshape(n, -1), u[0, :, s0:s0 + w], preferred_element_type=F32)
            l += jnp.dot(ct[1, h, j0:j1].reshape(n, -1), u[1, :, s0:s0 + w], preferred_element_type=F32)
            parts.append(l)
        return [jnp.concatenate([q[i * 32:(i + 1) * 32] for q in parts], axis=0) for i in range(j1 - j0)]

    def s0(k):
        w = WIDTHS[k]
        ys[k, 0, :, 0:w] = low(0, 1, k)[0].astype(BF16)
        y_copies(k)[0].start()

    def s1(k):
        s0, w = STARTS[k], WIDTHS[k]
        up, dn, own = low(1, 4, k)
        relayed, direct = (up, dn) if k % 2 == 0 else (dn, up)
        lf[:, s0:s0 + w] = own
        cps = y_copies(k)
        ys[k, 2, :, 0:w] = direct.astype(BF16)
        cps[2].start()
        cps[0].wait_recv()
        ys[k, 1, :, 0:w] = (relayed + yr[k, 0, :, 0:w].astype(F32)).astype(BF16)
        cps[1].start()

    def s2(k):
        s0, w = STARTS[k], WIDTHS[k]
        g = lf[:, s0:s0 + w]
        for i in (2, 1):
            y_copies(k)[i].wait_recv()
            g = g + yr[k, i, :, 0:w].astype(F32)
        for zz in range(NZ):
            part = g[zz * 8:(zz + 1) * 8]
            zf[zz, :, s0:s0 + w] = part
            zs[k, zz, :, 0:w // 2] = jnp.concatenate([part[:, :w // 2], part[:, w // 2:]], axis=0).astype(BF16)
        for cp in z_copies(k):
            cp.start()

    def step(k, g):
        s0, w = STARTS[k], WIDTHS[k]
        a, b, dr = adam_rows(mv[:, s0:s0 + w], vv[:, s0:s0 + w], g)
        nm[:, s0:s0 + w] = a
        nv[:, s0:s0 + w] = b
        db[k, c, y, z, :, 0:w // 2] = jnp.concatenate([dr[:, :w // 2], dr[:, w // 2:]], axis=0).astype(BF16)

    def s3(k):
        s0, w = STARTS[k], WIDTHS[k]
        got(zr.at[k, :, :, pl.ds(0, w // 2)], rz.at[k])
        t = zr[k, 0, :, 0:w // 2].astype(F32)
        for d in range(1, NZ - 1):
            t = t + zr[k, d, :, 0:w // 2].astype(F32)
        step(k, zf[z, :, s0:s0 + w] + jnp.concatenate([t[0:8], t[8:16]], axis=1))
        for cp in gz_copies(k):
            cp.start()

    def s4(k):
        got(zr.at[k, :, :, pl.ds(0, WIDTHS[k] // 2)], rg.at[k])
        for cp in gy_copies(k)[0]:
            cp.start()
        k_copies(k)[0].start()

    def s5(k):
        _, first_in, second = gy_copies(k)
        out = k_copies(k)
        first_in[0].wait_recv()
        second[0].start()
        first_in[1].wait_recv()
        second[1].start()
        out[3].start()
        out[1].start()

    def s6(k):
        got(db.at[k, c, 0, :, :, pl.ds(0, WIDTHS[k] // 2)], rh.at[k, 2])
        k_copies(k)[2].start()

    def qz_copies(k):
        w = pl.ds(0, WIDTHS[k])
        return [
            send(qs.at[k, zd[d], :, w], qr.at[k, d - 1, :, w], sqz, rqz.at[k], zdev[d])
            for d in range(1, NZ)
        ]

    def qy_copies(k):
        w = pl.ds(0, WIDTHS[k] // 2)
        return [
            send(qys.at[k, j, :, w], qyr.at[k, j, :, w], sqy, rqy.at[k], (ydev[2], ydev[1], ydev[3])[j])
            for j in range(3)
        ]

    def qg_copies(k):
        mine = db.at[k, c, y, z, :, pl.ds(0, WIDTHS[k] // 2)]
        return [send(mine, mine, sqg, rqg.at[k], ydev[d]) for d in range(1, NY)]

    def qh_copies(k):
        mine = db.at[k, c, :, z, :, pl.ds(0, WIDTHS[k] // 2)]
        return [send(mine, mine, sqh, rqh.at[k], zdev[d]) for d in range(1, NZ)]

    def got(ref, sem):
        send(ref, ref, sem, sem, sib).wait_recv()

    def left(ref, sem):
        send(ref, ref, sem, sem, sib).wait_send()

    def q1(k):
        s0, w = STARTS[k], WIDTHS[k]
        for h in range(2):
            l = jnp.dot(ct[0, h].reshape(128, -1), u[0, :, s0:s0 + w], preferred_element_type=F32)
            l += jnp.dot(ct[1, h].reshape(128, -1), u[1, :, s0:s0 + w], preferred_element_type=F32)
            for zl in range(4):
                part = jnp.concatenate([l[j * 32 + zl * 8:j * 32 + zl * 8 + 8] for j in range(NY)], axis=0)
                qf[k, h * 4 + zl, :, 0:w] = part
                qs[k, h * 4 + zl, :, 0:w] = part.astype(BF16)
        for cp in qz_copies(k):
            cp.start()

    def halves(part):
        w = part.shape[1] // 2
        return jnp.concatenate([part[:, :w], part[:, w:]], axis=0).astype(BF16)

    def q2(k):
        w = WIDTHS[k]
        got(qr.at[k, :, :, pl.ds(0, w)], rqz.at[k])
        g = qf[k, z, :, 0:w]
        for d in range(NZ - 1):
            g = g + qr[k, d, :, 0:w].astype(F32)
        qf[k, 0, 0:8, 0:w] = g[24:32]
        for j in range(3):
            qys[k, j, :, 0:w // 2] = halves(g[j * 8:j * 8 + 8])
        for cp in qy_copies(k):
            cp.start()

    def q3(k):
        w = WIDTHS[k]
        got(qyr.at[k, :, :, pl.ds(0, w // 2)], rqy.at[k])
        t = qyr[k, 0, :, 0:w // 2].astype(F32)
        for j in range(1, 3):
            t = t + qyr[k, j, :, 0:w // 2].astype(F32)
        step(k, qf[k, 0, 0:8, 0:w] + jnp.concatenate([t[0:8], t[8:16]], axis=1))
        for cp in qg_copies(k):
            cp.start()

    def q4(k):
        got(qyr.at[k, :, :, pl.ds(0, WIDTHS[k] // 2)], rqg.at[k])
        for cp in qh_copies(k):
            cp.start()

    def q5(k):
        got(db.at[k, c, :, pl.ds(0, NZ - 1), :, pl.ds(0, WIDTHS[k] // 2)], rqh.at[k])
        for cp in k_copies(k):
            cp.start()

    def s7(k):
        s0, w = STARTS[k], WIDTHS[k]
        got(db.at[k, oc, :, :, :, pl.ds(0, w // 2)], rk.at[k])
        d_all = db[k, :, :, :, :, 0:w // 2].reshape(1024, w // 2)
        for s in range(2):
            o = s0 + s * (w // 2)
            wo[:, o:o + w // 2] = 0.25 * jnp.dot(be[s], d_all, preferred_element_type=F32)

    x_reduce(0)
    x_reduce(1)
    lu.wait()
    cu_in.wait_recv()
    x_gathered(0)
    for k in range(NQ, NCH):
        s0(k)
    x_gathered(1)
    lm.wait()
    lv.wait()
    basis_send()

    p_stages = ((s1, P1), (s2, P2), (s3, P3), (s4, P4), (s5, P5), (s6, P6), (s7, 0.0))
    q_stages = ((q1, Q1), (q2, Q2), (q3, Q3), (q4, Q4), (q5, Q5), (s7, 0.0))
    order = [(BASIS_AT, 0, 0, lambda k: basis_columns())]
    for k in range(NCH):
        t = Q_PACE * k if k < NQ else P_PACE * (k - NQ) + P_START
        for i, (stage, latency) in enumerate(q_stages if k < NQ else p_stages):
            order.append((t, -i, k, stage))
            t += latency
    for _, _, k, stage in sorted(order, key=lambda e: e[:3]):
        stage(k)

    for p in range(2):
        left(xr.at[:, PARTS[p]], sx.at[p])
        for d in range(1, NX):
            q_copies(p)[d].wait_send()

        @pl.when(cq != c)
        def _():
            q_copies(p)[0].wait_send()

    cu.wait_send()

    @pl.when(x == y)
    def _():
        for cp in cbs:
            cp.wait_send()

    for k in range(NCH):
        w, half = pl.ds(0, WIDTHS[k]), pl.ds(0, WIDTHS[k] // 2)
        if k < NQ:
            left(qr.at[k, :, :, w], sqz)
            left(qyr.at[k, :, :, half], sqy)
            left(qyr.at[k, :, :, half], sqg)
            left(db.at[k, 0, :, pl.ds(0, NZ - 1), :, half], sqh)
        else:
            left(ys.at[k, :, :, w], sy)
            left(zr.at[k, :, :, half], sz)
            left(zr.at[k, :, :, half], sg)
            left(db.at[k, 0, pl.ds(0, 3), :, :, half], sh)
        left(db.at[k, 0, :, :, :, half], sk)


def body(features, up_cotangent, proj_basis, first_moment, second_moment):
    tok, feat = features.shape
    depth, rank = proj_basis.shape
    cols = up_cotangent.shape[1]
    kw = feat // KB
    rows = 128
    dma = pltpu.SemaphoreType.DMA
    anyspec = pl.BlockSpec(memory_space=pl.ANY)
    wu, nf, ns = pl.pallas_call(
        kernel,
        out_shape=(
            pltpu.VMEM((rows, cols), F32),
            pltpu.VMEM(first_moment.shape, F32),
            pltpu.VMEM(second_moment.shape, F32),
        ),
        in_specs=[anyspec] * 5,
        out_specs=(pl.BlockSpec(memory_space=pltpu.VMEM),) * 3,
        scratch_shapes=[
            pltpu.VMEM((KB, tok, kw), BF16),
            pltpu.VMEM((KB, kw, rank), BF16),
            pltpu.VMEM((2, tok, cols), BF16),
            pltpu.VMEM((8, cols), F32),
            pltpu.VMEM((8, cols), F32),
            pltpu.VMEM((tok, rank), F32),
            pltpu.VMEM((NX, NY, 32, tok), F32),
            pltpu.VMEM((NX, NY, 32, tok), BF16),
            pltpu.VMEM((NX - 1, NY, 32, tok), BF16),
            pltpu.VMEM((NY, 32, tok), BF16),
            pltpu.VMEM((2, 2, NY, 32, tok), BF16),
            pltpu.VMEM((NQ, NZ, 32, WMAX), BF16),
            pltpu.VMEM((NQ, NZ - 1, 32, WMAX), BF16),
            pltpu.VMEM((NQ, NZ, 32, WMAX), F32),
            pltpu.VMEM((NQ, 3, 16, WMAX // 2), BF16),
            pltpu.VMEM((NQ, 3, 16, WMAX // 2), BF16),
            pltpu.VMEM((64, cols), F32),
            pltpu.VMEM((NCH, 3, 64, WMAX), BF16),
            pltpu.VMEM((NCH, 3, 64, WMAX), BF16),
            pltpu.VMEM((NZ, 8, cols), F32),
            pltpu.VMEM((NCH, NZ, 16, WMAX // 2), BF16),
            pltpu.VMEM((NCH, NZ - 1, 16, WMAX // 2), BF16),
            pltpu.VMEM((NCH, 2, NY, NZ, 16, WMAX // 2), BF16),
            pltpu.VMEM((rows, rank), BF16),
            pltpu.VMEM((2, rows, 2 * rank), BF16),
            dma((KB,)), dma((KB,)), dma(()), dma((2,)),
            dma((2,)), dma((2,)), dma((2, 4)), dma((2, 2, 2)), dma(()), dma(()), dma((3,)), dma(()),
            dma(()), dma((NCH, 3)), dma(()), dma((NCH,)), dma(()), dma((NCH,)),
            dma(()), dma((NCH, 3)), dma(()), dma((NCH,)),
            dma(()), dma((NQ,)), dma(()), dma((NQ,)), dma(()), dma((NQ,)), dma(()), dma((NQ,)),
        ],
        compiler_params=pltpu.CompilerParams(
            collective_id=0, has_side_effects=True, vmem_limit_bytes=56 * 2**20
        ),
        cost_estimate=pl.CostEstimate(flops=4 * 10**9, bytes_accessed=12 * 10**6, transcendentals=0),
        name="galore",
    )(features, up_cotangent, proj_basis, first_moment, second_moment)
    return (wu, nf, ns)


def solution(mesh):
    return jax.shard_map(
        body,
        mesh=mesh,
        in_specs=(P("dp", "mp"), P("dp", "mp"), P("mp", None), P("dp", "mp"), P("dp", "mp")),
        out_specs=(P("dp", "mp"), P("dp", "mp"), P("dp", "mp")),
        check_vma=False,
    )
```
